256 devices in a mesh: ctx: 16 (over z_lo, x, core), head: 16 (over y, z_hi).
Axes of the slice: x: 4, y: 4, z: 8 (z_hi: 4, z_lo: 2; z = z_hi * 2 + z_lo), core: 2. Of those that a mesh axis runs over, the one named last changes fastest.
Arguments:
- queries: bfloat16 [4096, 64, 576], P('ctx', 'head'), may hold values from -22 to 22
- latent: bfloat16 [4096, 576], P('ctx'), may hold values from -4 to 4
- grad_out: bfloat16 [4096, 64, 512], P('ctx', 'head'), may hold values from -24 to 24
- advantage: float32 [4096], P('ctx'), may hold values from -4 to 4
- ancestors: int32 [32, 8], P('ctx'), may hold values from -1 to 30, as said below
Outputs:
- query_grad: bfloat16 [4096, 64, 576], P(('ctx', 'head'))
- latent_grad: float32 [4096, 576], P(('ctx', 'head'))
The draws below stay inside these ranges and needn't reach their ends.
Inputs may be any that keep to these rules, and one draw needn't show every extreme that they name: Row b lists ancestors of block b, nearest first: the first entry is the parent of b, each later entry the parent of the one before; after the chain ends or after 8 entries the row holds -1. Entries are always earlier blocks. Block 30 has as parent the block 16 earlier, and block 31 has block 30 as parent.
All inputs are finite; a program needn't handle non-finite values.
Results may differ from the reference program's by a relative error of at most 0.012.
Values may be sent and summed in bfloat16 or wider, within the bound.
No kernel may reach another device: no remote copies, remote signals or barrier semaphores. Data moves between devices by JAX's collectives and lax.ppermute only.
A program may use at most 128 MiB of HBM per device.

```python
import jax
import jax.numpy as jnp
from jax import lax

LAT = 512
QW = 576
HEADS = 64
BLK = 128
NLIST = 8
TOKENS = 4096


def shared_latent(key):
    return jnp.clip(jax.random.normal(key, (TOKENS, QW), jnp.float32), -4.0, 4.0)


def draw_latent(key, part):
    base = shared_latent(key)
    result = base
    return result.astype(jnp.bfloat16)


def draw_queries(key, part):
    key = jax.random.fold_in(key, 12)
    first_key = jax.random.fold_in(key, 0)
    result = jnp.clip(jax.random.normal(first_key, (TOKENS, HEADS, QW), jnp.float32), -4.0, 4.0)
    return result.astype(jnp.bfloat16)


def draw_ancestors(key, part):
    key = jax.random.fold_in(key, 13)
    jump_key, root_key = jax.random.split(key)
    block_count = TOKENS // BLK
    blocks = jnp.arange(block_count, dtype=jnp.int32)
    jumps = jax.random.randint(jump_key, (block_count,), 1, 4)
    roots = jax.random.randint(root_key, (block_count,), 0, 5) == 0
    parent = jnp.where(roots, -1, blocks - jumps)
    parent = jnp.where(parent < 0, -1, parent)
    forced = blocks >= block_count - NLIST - 1
    parent = jnp.where(forced & (blocks >= 1), blocks - 1, parent)
    far_block = block_count - 2 - block_count // 2
    parent = jnp.where(blocks == block_count - 2, far_block, parent).astype(jnp.int32)
    current = parent
    columns = []
    for slot in range(NLIST):
        columns.append(current)
        current = jnp.where(current >= 0, parent[jnp.maximum(current, 0)], -1).astype(jnp.int32)
    return jnp.stack(columns, axis=1).astype(jnp.int32)


def level_of(own_key, shape, pieces, least, top_value):
    def one(dim, parts):
        steps = jax.random.uniform(jax.random.fold_in(jax.random.fold_in(own_key, 6), dim), (parts,), jnp.float32, least / len(pieces), top_value / len(pieces))
        return jnp.repeat(jnp.exp(steps), shape[dim] // parts).reshape((-1,) + (1,) * (len(shape) - dim - 1))

    level = one(*pieces[0])
    for cut in pieces[1:]:
        level = level * one(*cut)
    return level


def bell_draw(stream_key, shape, spread, reach, shards=(), kind=jnp.bfloat16):
    loudness = level_of(stream_key, shape, shards, -0.22, 0.18) if shards else 1.0
    values = jax.random.normal(stream_key, shape, jnp.float32) * spread * loudness
    return jnp.minimum(jnp.maximum(values, -reach), reach).astype(kind)


def setup_inputs(seed: int = 0) -> dict:
    key_of = jax.random.split(jax.random.key(seed), 6)
    return {
        "queries": draw_queries(jax.random.fold_in(key_of[5], 71), 0),
        "latent": draw_latent(jax.random.fold_in(key_of[5], 71), 0),
        "grad_out": bell_draw(key_of[2], (TOKENS, HEADS, LAT), 4.0, 24.0, ((0, 16), (1, 16))),
        "advantage": bell_draw(key_of[3], (TOKENS,), 1.0, 4.0, ((0, 16),), jnp.float32),
        "ancestors": draw_ancestors(jax.random.fold_in(key_of[5], 71), 0),
    }


SOFTMAX_SCALE = 0.07216878364870322


def block_grads(q_block, g_block, lists, own, key_blocks):
    slots = jnp.concatenate([own[:, None], lists], axis=1).astype(jnp.int32)
    present = jnp.concatenate([jnp.ones_like(own[:, None]), (lists >= 0).astype(jnp.int32)], axis=1)
    safe_index = jnp.maximum(slots, 0)
    count_q = slots.shape[0]
    count_s = slots.shape[1]
    width = key_blocks.shape[2]
    keys = key_blocks[safe_index].reshape(count_q, count_s * BLK, width)
    scores = jnp.einsum('qihd,qjd->qhij', q_block.astype(jnp.float32), keys.astype(jnp.float32)) * SOFTMAX_SCALE
    column = jnp.arange(count_s * BLK)
    slot_of = column // BLK
    inner = column % BLK
    row_pos = jnp.arange(BLK)
    diagonal = (slot_of[None, :] == 0) & (inner[None, :] <= row_pos[:, None])
    listed = (slot_of[None, :] > 0) & (present[:, slot_of] > 0)
    visible = (diagonal[None, :, :] | listed[:, None, :])[:, None, :, :]
    masked = jnp.where(visible, scores, jnp.float32(-1e30))
    top_score = jnp.max(masked, axis=-1, keepdims=True)
    expo = jnp.where(visible, jnp.exp(masked - top_score), jnp.float32(0.0))
    probs = expo / jnp.sum(expo, axis=-1, keepdims=True)
    probs_low = probs.astype(jnp.bfloat16)
    values = keys[:, :, :LAT]
    dprobs = jnp.einsum('qihc,qjc->qhij', g_block.astype(jnp.float32), values.astype(jnp.float32))
    delta = jnp.sum(probs * dprobs, axis=-1, keepdims=True)
    dscores = (probs * (dprobs - delta) * SOFTMAX_SCALE).astype(jnp.bfloat16)
    query_part = jnp.einsum('qhij,qjd->qihd', dscores.astype(jnp.float32), keys.astype(jnp.float32)).astype(jnp.bfloat16)
    key_part = jnp.einsum('qhij,qihd->qjd', dscores.astype(jnp.float32), q_block.astype(jnp.float32))
    value_part = jnp.einsum('qhij,qihc->qjc', probs_low.astype(jnp.float32), g_block.astype(jnp.float32))
    padding = jnp.zeros((count_q, count_s * BLK, width - LAT), jnp.float32)
    contrib = (key_part + jnp.concatenate([value_part, padding], axis=-1)).reshape(count_q, count_s, BLK, width)
    block_count = key_blocks.shape[0]
    onehot = ((safe_index[:, :, None] == jnp.arange(block_count, dtype=jnp.int32)[None, None, :]) & (present[:, :, None] > 0)).astype(jnp.float32)
    term = jnp.einsum('qsn,qsbd->nbd', onehot, contrib, precision=lax.Precision.HIGHEST)
    return query_part, term


def reference(queries, latent, grad_out, advantage, ancestors):
    block_count = TOKENS // BLK
    key_blocks = latent.reshape(block_count, BLK, QW)
    weighted = (advantage[:, None, None] * grad_out.astype(jnp.float32)).astype(jnp.bfloat16)
    q_blocks = queries.reshape(block_count, 1, BLK, HEADS, QW)
    g_blocks = weighted.reshape(block_count, 1, BLK, HEADS, LAT)
    list_rows = ancestors.reshape(block_count, 1, NLIST)
    own_rows = jnp.arange(block_count, dtype=jnp.int32).reshape(block_count, 1)

    def advance(total, items):
        q_block, g_block, lists, own = items
        query_part, term = block_grads(q_block, g_block, lists, own, key_blocks)
        return total + term, query_part

    start = jnp.zeros((block_count, BLK, QW), jnp.float32)
    total, query_parts = lax.scan(advance, start, (q_blocks, g_blocks, list_rows, own_rows))
    return query_parts.reshape(TOKENS, HEADS, QW), total.reshape(TOKENS, QW)
```

```python
import jax
import jax.numpy as jnp
from jax import lax
from jax.experimental import pallas as pl
from jax.experimental.pallas import tpu as pltpu
from jax.sharding import Mesh
from jax.sharding import PartitionSpec as P

LAT = 512
QW = 576
BLK = 128
NSLOT = 9
HALF = 16

SOFTMAX_SCALE = 0.07216878364870322
LOG2E = 1.4426950408889634
MASKED = -1e30

SPLIT = (("z_lo", 2), ("x", 4), ("core", 2), ("y", 4), ("z_hi", 4))
CTX = ("z_lo", "x", "core")
HEAD = ("y", "z_hi")


def kernel(info, qt_ref, g_ref, mine_ref, other_ref, dq_ref, keep_ref, send_ref, keys, acc):
    block, pair = pl.program_id(0), pl.program_id(1)

    @pl.when((block == 0) & (pair == 0))
    def _():
        def clear(i, carry):
            acc[i] = jnp.zeros((BLK, QW), jnp.float32)
            return carry

        lax.fori_loop(0, 2 * HALF, clear, 0)

    @pl.when(pair == 0)
    def _():
        for s in range(NSLOT):
            place = info[block, s]
            rows = pl.ds(s * BLK, BLK)

            @pl.when(place < HALF)
            def _():
                keys[rows, :] = mine_ref[place]

            @pl.when(place >= HALF)
            def _():
                keys[rows, :] = other_ref[place - HALF]

    k = keys[...]
    qt = jnp.concatenate([qt_ref[0], qt_ref[1]], axis=1)
    g = g_ref[...].reshape(2 * BLK, LAT)
    nt = (((1,), (1,)), ((), ()))
    scores = jnp.dot(k, qt, preferred_element_type=jnp.float32)
    dprobs = lax.dot_general(k[:, :LAT], g, nt, preferred_element_type=jnp.float32)

    key_pos = lax.broadcasted_iota(jnp.int32, (BLK, 2 * BLK), 0)
    row_pos = lax.broadcasted_iota(jnp.int32, (BLK, 2 * BLK), 1) % BLK
    parts = []
    for s in range(NSLOT):
        part = scores[s * BLK : (s + 1) * BLK] * (SOFTMAX_SCALE * LOG2E)
        if s == 0:
            part = jnp.where(key_pos <= row_pos, part, MASKED)
        else:
            part = jnp.where(info[block, NSLOT + s] > 0, part, MASKED)
        parts.append(part)
    masked = jnp.concatenate(parts, axis=0)
    top = jnp.max(masked, axis=0, keepdims=True)
    expo = jnp.exp2(masked - top)
    probs = expo * (1.0 / jnp.sum(expo, axis=0, keepdims=True))
    delta = jnp.sum(probs * dprobs, axis=0, keepdims=True)
    dscores = (probs * (dprobs - delta) * SOFTMAX_SCALE).astype(jnp.bfloat16)
    low = probs.astype(jnp.bfloat16)

    dq = lax.dot_general(
        dscores, k, (((0,), (0,)), ((), ())), preferred_element_type=jnp.float32
    ).astype(jnp.bfloat16)
    dq_ref[:, 0] = dq[:BLK].reshape(8, 16, QW)
    dq_ref[:, 1] = dq[BLK:].reshape(8, 16, QW)

    key_part = lax.dot_general(dscores, qt, nt, preferred_element_type=jnp.float32)
    value_part = jnp.dot(low, g, preferred_element_type=jnp.float32)
    for s in range(NSLOT):
        place = info[block, s]
        rows = slice(s * BLK, (s + 1) * BLK)
        acc[place, :, :LAT] += key_part[rows, :LAT] + value_part[rows]
        acc[place, :, LAT:] += key_part[rows, LAT:]

    @pl.when((block == 1) & (pair == 1))
    def _():
        def write(i, carry):
            keep_ref[i] = acc[i].astype(jnp.bfloat16)
            send_ref[i] = acc[HALF + i].astype(jnp.bfloat16)
            return carry

        lax.fori_loop(0, HALF, write, 0)


def local_grads(info, qt, weighted, mine, other):
    whole = lambda b, p, info: (0, 0, 0)
    return pl.pallas_call(
        kernel,
        grid_spec=pltpu.PrefetchScalarGridSpec(
            num_scalar_prefetch=1,
            grid=(2, 2),
            in_specs=[
                pl.BlockSpec((2, QW, BLK), lambda b, p, info: (p, 0, b)),
                pl.BlockSpec((2, BLK, LAT), lambda b, p, info: (p, b, 0)),
                pl.BlockSpec((HALF, BLK, QW), whole, pipeline_mode=pl.Buffered(1)),
                pl.BlockSpec((HALF, BLK, QW), whole, pipeline_mode=pl.Buffered(1)),
            ],
            out_specs=[
                pl.BlockSpec((8, 2, 16, QW), lambda b, p, info: (b, p, 0, 0)),
                pl.BlockSpec((HALF, BLK, QW), whole),
                pl.BlockSpec((HALF, BLK, QW), whole),
            ],
            scratch_shapes=[
                pltpu.VMEM((NSLOT * BLK, QW), jnp.bfloat16),
                pltpu.VMEM((2 * HALF, BLK, QW), jnp.float32),
            ],
        ),
        out_shape=[
            jax.ShapeDtypeStruct((16, 4, 16, QW), jnp.bfloat16),
            jax.ShapeDtypeStruct((HALF, BLK, QW), jnp.bfloat16),
            jax.ShapeDtypeStruct((HALF, BLK, QW), jnp.bfloat16),
        ],
        compiler_params=pltpu.CompilerParams(
            dimension_semantics=("arbitrary", "arbitrary"),
            vmem_limit_bytes=56 * 1024 * 1024,
        ),
    )(info, qt, weighted, mine, other)


def swap_cores(a):
    return lax.ppermute(a, "core", [(0, 1), (1, 0)])


def exchange(a, axes):
    return lax.all_to_all(a, axes, split_axis=0, concat_axis=0, tiled=True)


def on_device(queries, latent, grad_out, advantage, ancestors):
    core = lax.axis_index("core")
    mine = exchange(jnp.broadcast_to(latent[None], (8, 256, QW)), ("x", "z_lo"))
    mine = mine.reshape(HALF, BLK, QW)
    other = swap_cores(mine)

    qt = jnp.transpose(queries, (1, 2, 0))
    weighted = (advantage[:, None, None] * grad_out.astype(jnp.float32)).astype(jnp.bfloat16)
    weighted = jnp.transpose(weighted, (1, 0, 2))

    own = lax.axis_index(CTX) * 2 + jnp.arange(2, dtype=jnp.int32)
    slots = jnp.concatenate([own[:, None], ancestors], axis=1)
    present = (slots >= 0).astype(jnp.int32)
    n = jnp.maximum(slots, 0)
    z_lo, x, owner_core, parity = n // 16, (n // 4) % 4, (n // 2) % 2, n % 2
    place = jnp.where(owner_core == core, 0, HALF) + x * 4 + z_lo * 2 + parity
    info = jnp.concatenate([place, present], axis=1)

    dq, keep, send = local_grads(info, qt, weighted, mine, other)

    total = keep.astype(jnp.float32) + swap_cores(send).astype(jnp.float32)
    rows = exchange(total.astype(jnp.bfloat16).reshape(2048, QW), "x")
    rows = jnp.sum(rows.reshape(4, 512, QW).astype(jnp.float32), axis=0).astype(jnp.bfloat16)
    rows = exchange(rows, ("z_lo",) + HEAD)
    latent_grad = jnp.sum(rows.reshape(32, 16, QW).astype(jnp.float32), axis=0)

    dq = exchange(dq, HEAD)
    query_grad = jnp.transpose(dq.reshape(64, 16, QW), (1, 0, 2))
    return query_grad, latent_grad


def solution(mesh):
    names = tuple(name for name, _ in SPLIT)
    sizes = tuple(size for _, size in SPLIT)
    fine = Mesh(mesh.devices.reshape(sizes), names)
    in_specs = (P(CTX, HEAD, None), P(CTX, None), P(CTX, HEAD, None), P(CTX), P(CTX, None))
    out_specs = (P(CTX + HEAD, None, None), P(CTX + HEAD, None))
    return jax.shard_map(
        on_device, mesh=fine, in_specs=in_specs, out_specs=out_specs, check_vma=False
    )
```

```python
import functools
import math

import jax
import jax.numpy as jnp
from jax import lax
from jax.experimental import pallas as pl
from jax.experimental.pallas import tpu as pltpu
from jax.sharding import Mesh
from jax.sharding import PartitionSpec as P

LAT = 512
QW = 576
BLK = 128
NSLOT = 9
NB = 32
HEADS_HERE = 4
MIB = 1024 * 1024
ROWS = HEADS_HERE * BLK

SOFTMAX_SCALE = 0.07216878364870322
LOG2E = 1.4426950408889634
MASKED = -1e30

SPLIT = (("z_lo", 2), ("x", 4), ("core", 2), ("y", 4), ("z_hi", 4))
AXES = tuple(name for name, _ in SPLIT)
SIZES = tuple(size for _, size in SPLIT)
CTX = AXES[:3]
HEAD = AXES[3:]


def kernel(info, q_ref, qt_ref, g_ref, gt_ref, *rest, npieces, nouts):
    pieces, rest = rest[:npieces], rest[npieces:]
    dq_ref, outs = rest[0], rest[1 : 1 + nouts]
    all_keys, keys, dense, sem, out_sem = rest[1 + nouts :]
    b = pl.program_id(0)
    each = NB // nouts

    def writes():
        return [
            pltpu.make_async_copy(dense.at[pl.ds(i * each, each)], out, out_sem)
            for i, out in enumerate(outs)
        ]

    @pl.when(b == 0)
    def _():
        copies, at = [], 0
        for piece in pieces:
            n = piece.shape[0]
            copies.append(pltpu.make_async_copy(piece, all_keys.at[pl.ds(at, n)], sem))
            at += n
        for copy in copies:
            copy.start()

        def clear(i, carry):
            dense[i] = jnp.zeros((QW, BLK), jnp.bfloat16)
            return carry

        lax.fori_loop(0, NB, clear, 0)
        for copy in copies:
            copy.wait()

    for s in range(NSLOT):
        keys[:, s * BLK : (s + 1) * BLK] = all_keys[info[b, s]]
    k = keys[...]
    q = q_ref[...].reshape(ROWS, QW)
    g = g_ref[...].reshape(ROWS, LAT)
    scores = jnp.dot(q, k, preferred_element_type=jnp.float32)
    dprobs = jnp.dot(g, k[:LAT], preferred_element_type=jnp.float32)

    row_pos = lax.broadcasted_iota(jnp.int32, (ROWS, BLK), 0) % BLK
    key_pos = lax.broadcasted_iota(jnp.int32, (ROWS, BLK), 1)
    parts = []
    for s in range(NSLOT):
        part = scores[:, s * BLK : (s + 1) * BLK] * (SOFTMAX_SCALE * LOG2E)
        if s == 0:
            part = jnp.where(key_pos <= row_pos, part, MASKED)
        else:
            part = jnp.where(info[b, NSLOT + s] > 0, part, MASKED)
        parts.append(part)
    masked = jnp.concatenate(parts, axis=1)
    top = jnp.max(masked, axis=1, keepdims=True)
    expo = jnp.exp2(masked - top)
    probs = expo * (1.0 / jnp.sum(expo, axis=1, keepdims=True))
    delta = jnp.sum(probs * dprobs, axis=1, keepdims=True)
    dscores = (probs * (dprobs - delta) * SOFTMAX_SCALE).astype(jnp.bfloat16)
    low = probs.astype(jnp.bfloat16)

    qt = jnp.concatenate([qt_ref[h] for h in range(HEADS_HERE)], axis=1)
    gt = jnp.concatenate([gt_ref[h] for h in range(HEADS_HERE)], axis=1)
    key_part = jnp.dot(qt, dscores, preferred_element_type=jnp.float32)
    value_part = jnp.dot(gt, low, preferred_element_type=jnp.float32)
    for s in range(NSLOT):
        cols = slice(s * BLK, (s + 1) * BLK)
        dest = info[b, 2 * NSLOT + s]
        head = dense[dest, :LAT].astype(jnp.float32) + key_part[:LAT, cols] + value_part[:, cols]
        tail = dense[dest, LAT:].astype(jnp.float32) + key_part[LAT:, cols]
        dense[dest, :LAT] = head.astype(jnp.bfloat16)
        dense[dest, LAT:] = tail.astype(jnp.bfloat16)

    @pl.when(b == 1)
    def _():
        for copy in writes():
            copy.start()

    dq = lax.dot_general(
        dscores, k, (((1,), (1,)), ((), ())), preferred_element_type=jnp.float32
    ).astype(jnp.bfloat16)
    for h in range(HEADS_HERE):
        dq_ref[:, h] = dq[h * BLK : (h + 1) * BLK].reshape(8, 16, QW)

    @pl.when(b == 1)
    def _():
        for copy in writes():
            copy.wait()


def local_grads(info, q, qt, g, gt, pieces, nouts):
    each = NB // nouts
    return pl.pallas_call(
        functools.partial(kernel, npieces=len(pieces), nouts=nouts),
        grid_spec=pltpu.PrefetchScalarGridSpec(
            num_scalar_prefetch=1,
            grid=(2,),
            in_specs=[
                pl.BlockSpec((HEADS_HERE, BLK, QW), lambda b, info: (0, b, 0)),
                pl.BlockSpec((HEADS_HERE, QW, BLK), lambda b, info: (0, 0, b)),
                pl.BlockSpec((HEADS_HERE, BLK, LAT), lambda b, info: (0, b, 0)),
                pl.BlockSpec((HEADS_HERE, LAT, BLK), lambda b, info: (0, 0, b)),
            ]
            + [pl.BlockSpec(memory_space=pltpu.HBM)] * len(pieces),
            out_specs=[pl.BlockSpec((8, HEADS_HERE, 16, QW), lambda b, info: (b, 0, 0, 0))]
            + [pl.BlockSpec(memory_space=pltpu.HBM)] * nouts,
            scratch_shapes=[
                pltpu.VMEM((NB, QW, BLK), jnp.bfloat16),
                pltpu.VMEM((QW, NSLOT * BLK), jnp.bfloat16),
                pltpu.VMEM((NB, QW, BLK), jnp.bfloat16),
                pltpu.SemaphoreType.DMA,
                pltpu.SemaphoreType.DMA,
            ],
        ),
        out_shape=[jax.ShapeDtypeStruct((16, HEADS_HERE, 16, QW), jnp.bfloat16)]
        + [jax.ShapeDtypeStruct((each, QW, BLK), jnp.bfloat16)] * nouts,
        compiler_params=pltpu.CompilerParams(
            dimension_semantics=("arbitrary",), vmem_limit_bytes=56 * MIB
        ),
    )(info, q, qt, g, gt, *pieces)


def neighbour(x=0, y=0, z=0, core=0):
    pairs = []
    shape = dict(SPLIT)
    strides = {}
    step = 1
    for name in reversed(AXES):
        strides[name] = step
        step *= shape[name]
    for zl in range(shape["z_lo"]):
        for px in range(shape["x"]):
            for pc in range(shape["core"]):
                for py in range(shape["y"]):
                    for zh in range(shape["z_hi"]):

                        def index(zz, xx, cc, yy):
                            zz %= shape["z_lo"] * shape["z_hi"]
                            high, low = zz // shape["z_lo"], zz % shape["z_lo"]
                            return (
                                low * strides["z_lo"]
                                + (xx % shape["x"]) * strides["x"]
                                + (cc % 2) * strides["core"]
                                + (yy % shape["y"]) * strides["y"]
                                + high * strides["z_hi"]
                            )

                        zz = zh * shape["z_lo"] + zl
                        pairs.append((index(zz, px, pc, py), index(zz + z, px + x, pc + core, py + y)))
    return pairs


def other_z():
    shape = tuple(size for _, size in SPLIT)
    step = math.prod(shape[1:])
    return [(i, (i + step) % (2 * step)) for i in range(2 * step)]


ALONG_X = [neighbour(x=d) for d in range(4)]
ALONG_Y = [neighbour(y=d) for d in range(4)]
RIGHT, LEFT = ALONG_X[1], ALONG_X[3]
UP, DOWN = neighbour(z=1), neighbour(z=-1)
SWAP = neighbour(core=1)
OTHER_Z = other_z()


def move(a, pairs):
    return lax.ppermute(a, AXES, pairs)


def pack_kernel(*refs):
    *pieces, out, sem = refs
    copies, at = [], 0
    for piece in pieces:
        n = piece.shape[0]
        copies.append(pltpu.make_async_copy(piece, out.at[pl.ds(at, n)], sem))
        at += n
    for copy in copies:
        copy.start()
    for copy in copies:
        copy.wait()


def pack(pieces):
    n = sum(piece.shape[0] for piece in pieces)
    return pl.pallas_call(
        pack_kernel,
        in_specs=[pl.BlockSpec(memory_space=pl.ANY)] * len(pieces),
        out_specs=pl.BlockSpec(memory_space=pl.ANY),
        out_shape=jax.ShapeDtypeStruct((n, QW, BLK), jnp.bfloat16),
        scratch_shapes=[pltpu.SemaphoreType.DMA],
        compiler_params=pltpu.CompilerParams(vmem_limit_bytes=4 * MIB),
    )(*pieces)


PLACES = (0, 2, 8, 4, 6, 12, 10, 14)


def gather_keys(own, beside):
    across = move(own, ALONG_X[2])
    first = move(own, RIGHT), move(own, LEFT), move(own, OTHER_Z)
    (from_left, from_right, z_own), beside = lax.optimization_barrier((first, beside))
    z_across, z_left, z_right = move(z_own, ALONG_X[2]), move(from_left, UP), move(from_right, DOWN)
    near = pack([own, from_right, from_left, z_own])
    far = pack([across, z_across, z_right, z_left])
    return [near, far, move(near, SWAP), move(far, SWAP)], beside


def add_cores_kernel(keep, got, *rest):
    outs, (ours, theirs, total, in_sems, out_sem) = rest[:4], rest[4:]
    loads, writes = [], []
    for i, d in enumerate((2, 1, 3, 0)):
        part = pl.ds(4 * d, 4)
        loads.append(
            [
                pltpu.make_async_copy(keep.at[part], ours.at[part], in_sems.at[i]),
                pltpu.make_async_copy(got.at[part], theirs.at[part], in_sems.at[4 + i]),
            ]
        )
        for load in loads[-1]:
            load.start()
    for i, d in enumerate((2, 1, 3, 0)):
        for load in loads[i]:
            load.wait()
        part = slice(4 * d, 4 * d + 4)
        added = ours[part].astype(jnp.float32) + theirs[part].astype(jnp.float32)
        total[part] = added.astype(jnp.bfloat16)
        writes.append(pltpu.make_async_copy(total.at[pl.ds(4 * d, 4)], outs[d], out_sem))
        writes[-1].start()
    for write in writes:
        write.wait()


def add_cores(keep, got):
    hbm = pl.BlockSpec(memory_space=pltpu.HBM)
    return pl.pallas_call(
        add_cores_kernel,
        in_specs=[hbm, hbm],
        out_specs=[hbm] * 4,
        scratch_shapes=[pltpu.VMEM((16, QW, BLK), jnp.bfloat16)] * 3
        + [pltpu.SemaphoreType.DMA((8,)), pltpu.SemaphoreType.DMA],
        out_shape=[jax.ShapeDtypeStruct((4, QW, BLK), jnp.bfloat16)] * 4,
        compiler_params=pltpu.CompilerParams(vmem_limit_bytes=24 * MIB),
    )(keep, got)


def total_of(refs, index):
    return sum(ref[index].astype(jnp.float32) for ref in refs)


def add_x_kernel(y_ref, *refs):
    parts, outs, turned = refs[:4], refs[4:8], refs[8]
    for z in range(2):
        for block in range(2):
            rows = total_of(parts, 2 * z + block).T.astype(jnp.bfloat16)
            turned[2 * block, z] = rows[: BLK // 2]
            turned[2 * block + 1, z] = rows[BLK // 2 :]
    for d in range(4):
        outs[d][...] = turned[(y_ref[0] + d) & 3]


def add_x(my_y, parts):
    vmem = pl.BlockSpec(memory_space=pltpu.VMEM)
    shape = (2, BLK // 2, QW)
    return pl.pallas_call(
        add_x_kernel,
        grid_spec=pltpu.PrefetchScalarGridSpec(
            num_scalar_prefetch=1,
            grid=(),
            in_specs=[vmem] * 4,
            out_specs=[vmem] * 4,
            scratch_shapes=[pltpu.VMEM((4, *shape), jnp.bfloat16)],
        ),
        out_shape=[jax.ShapeDtypeStruct(shape, jnp.bfloat16)] * 4,
        compiler_params=pltpu.CompilerParams(vmem_limit_bytes=16 * MIB),
    )(my_y, *parts)


def add_y_kernel(*refs):
    *parts, out = refs
    out[...] = total_of(parts, ...).astype(jnp.bfloat16)


def add_y(parts):
    vmem = pl.BlockSpec(memory_space=pltpu.VMEM)
    return pl.pallas_call(
        add_y_kernel,
        in_specs=[vmem] * 4,
        out_specs=vmem,
        out_shape=jax.ShapeDtypeStruct((2, BLK // 2, QW), jnp.bfloat16),
        compiler_params=pltpu.CompilerParams(vmem_limit_bytes=8 * MIB),
    )(*parts)


def spread(parts, moves):
    return [parts[0]] + [move(parts[d], moves[d]) for d in (1, 2, 3)]


def on_device(queries, latent, grad_out, advantage, ancestors):
    weighted = (advantage[:, None, None] * grad_out.astype(jnp.float32)).astype(jnp.bfloat16)
    beside = (
        jnp.transpose(queries, (1, 0, 2)),
        jnp.transpose(queries, (1, 2, 0)),
        jnp.transpose(weighted, (1, 0, 2)),
        jnp.transpose(weighted, (1, 2, 0)),
    )
    own_keys = jnp.swapaxes(latent.reshape(2, BLK, QW), 1, 2)
    pieces, (q, qt, g, gt) = gather_keys(own_keys, beside)

    my_z, my_x, my_core = (lax.axis_index(name) for name in CTX)
    own = lax.axis_index(CTX) * 2 + jnp.arange(2, dtype=jnp.int32)
    slots = jnp.concatenate([own[:, None], ancestors], axis=1)
    present = (slots >= 0).astype(jnp.int32)
    n = jnp.maximum(slots, 0)
    z, x, c, block = n // 16, (n // 4) % 4, (n // 2) % 2, n % 2
    dz, dx, dc = z ^ my_z, (x - my_x) & 3, c ^ my_core
    offset = dz * 4 + dx
    place = dc * 16 + sum(jnp.where(offset == i, at, 0) for i, at in enumerate(PLACES)) + block
    dest = dc * 16 + dx * 4 + z * 2 + block
    info = jnp.concatenate([place, present, dest], axis=1)

    dq, keep, send = local_grads(info, q, qt, g, gt, pieces, 2)

    parts = spread(add_cores(keep, move(send, SWAP)), ALONG_X)
    parts = spread(add_x(lax.axis_index("y")[None], parts), ALONG_Y)
    rows = add_y(parts).reshape(128, QW)
    rows = lax.all_to_all(rows, ("z_lo", "z_hi"), split_axis=0, concat_axis=0, tiled=True)
    latent_grad = jnp.sum(rows.reshape(8, 16, QW).astype(jnp.float32), axis=0)

    dq = lax.all_to_all(dq, HEAD, split_axis=0, concat_axis=0, tiled=True)
    query_grad = jnp.transpose(dq.reshape(64, 16, QW), (1, 0, 2))
    return query_grad, latent_grad


def solution(mesh):
    fine = Mesh(mesh.devices.reshape(SIZES), AXES)
    in_specs = (P(CTX, HEAD, None), P(CTX, None), P(CTX, HEAD, None), P(CTX), P(CTX, None))
    out_specs = (P(CTX + HEAD, None, None), P(CTX + HEAD, None))
    return jax.shard_map(
        on_device, mesh=fine, in_specs=in_specs, out_specs=out_specs, check_vma=False
    )
```

```python
import functools
import math

import jax
import jax.numpy as jnp
from jax import lax
from jax.experimental import pallas as pl
from jax.experimental.pallas import tpu as pltpu
from jax.sharding import Mesh
from jax.sharding import PartitionSpec as P

LAT = 512
QW = 576
BLK = 128
NSLOT = 9
NB = 32
HEADS_HERE = 4
MIB = 1024 * 1024
ROWS = HEADS_HERE * BLK

SOFTMAX_SCALE = 0.07216878364870322
LOG2E = 1.4426950408889634
MASKED = -1e30

SPLIT = (("z_lo", 2), ("x", 4), ("core", 2), ("y", 4), ("z_hi", 4))
AXES = tuple(name for name, _ in SPLIT)
SIZES = tuple(size for _, size in SPLIT)
CTX = AXES[:3]
HEAD = AXES[3:]


def prepare_kernel(advantage_ref, qt_hbm, grad_hbm, q_hbm, g_hbm, gt_hbm, *scratch):
    qt, grad, q, g, gt, in_sems, out_sem = scratch
    heads = range(HEADS_HERE)
    load_grad = pltpu.make_async_copy(grad_hbm, grad, in_sems.at[HEADS_HERE])
    load_grad.start()
    loads = [pltpu.make_async_copy(qt_hbm.at[h], qt.at[h], in_sems.at[h]) for h in heads]
    for load in loads:
        load.start()
    writes = []

    def write(value, hbm, h):
        writes.append(pltpu.make_async_copy(value.at[h], hbm.at[h], out_sem))
        writes[-1].start()

    load_grad.wait()
    for h in heads:
        weighted = grad[:, h, :].T.astype(jnp.float32) * advantage_ref[...]
        gt[h] = weighted.astype(jnp.bfloat16)
        write(gt, gt_hbm, h)
        g[h] = gt[h].T
        write(g, g_hbm, h)
    for h in heads:
        loads[h].wait()
        q[h] = qt[h].T
        write(q, q_hbm, h)
    for copy in writes:
        copy.wait()


def prepare(qt, grad_out, advantage):
    hbm = pl.BlockSpec(memory_space=pltpu.HBM)
    shapes = (HEADS_HERE, 2 * BLK, QW), (HEADS_HERE, 2 * BLK, LAT), (HEADS_HERE, LAT, 2 * BLK)
    scratch = (qt.shape, grad_out.shape, *shapes)
    return pl.pallas_call(
        prepare_kernel,
        in_specs=[pl.BlockSpec(memory_space=pltpu.VMEM), hbm, hbm],
        out_specs=[hbm] * 3,
        out_shape=[jax.ShapeDtypeStruct(shape, jnp.bfloat16) for shape in shapes],
        scratch_shapes=[pltpu.VMEM(shape, jnp.bfloat16) for shape in scratch]
        + [pltpu.SemaphoreType.DMA((HEADS_HERE + 1,)), pltpu.SemaphoreType.DMA],
        compiler_params=pltpu.CompilerParams(vmem_limit_bytes=14 * MIB),
    )(advantage[None], qt, grad_out)


def kernel(info, q_hbm, qt_hbm, g_hbm, gt_hbm, *rest):
    pieces, rest = rest[:2], rest[2:]
    dq_ref, keep, send = rest[:3]
    q_ref, qt_ref, g_ref, gt_ref, slots, keys, dense, row_sems, slot_sems, out_sem = rest[3:]
    b = pl.program_id(0)

    def loads(block):
        rows = pl.ds(block * BLK, BLK)
        return [
            pltpu.make_async_copy(q_hbm.at[:, rows], q_ref.at[block], row_sems.at[block, 0]),
            pltpu.make_async_copy(g_hbm.at[:, rows], g_ref.at[block], row_sems.at[block, 1]),
            pltpu.make_async_copy(qt_hbm.at[:, :, rows], qt_ref.at[block], row_sems.at[block, 2]),
            pltpu.make_async_copy(gt_hbm.at[:, :, rows], gt_ref.at[block], row_sems.at[block, 3]),
        ]

    def slot_load(block, s, piece, at):
        return pltpu.make_async_copy(
            piece.at[at], slots.at[block, s], slot_sems.at[block, s]
        )

    @pl.when(b == 0)
    def _():
        for block in range(2):
            for s in range(NSLOT):
                place = info[block, s]
                first = 0
                for piece, count in zip(pieces, PIECES):

                    @pl.when((place >= first) & (place < first + count))
                    def _(piece=piece, first=first, s=s, block=block, place=place):
                        slot_load(block, s, piece, place - first).start()

                    first += count

            for load in loads(block):
                load.start()

        def clear(i, carry):
            dense[i] = jnp.zeros((QW, BLK), jnp.bfloat16)
            return carry

        lax.fori_loop(0, NB, clear, 0)

    for s in range(NSLOT):
        slot_load(b, s, pieces[0], 0).wait()
        keys[:, s * BLK : (s + 1) * BLK] = slots[b, s]
    k = keys[...]
    rows = loads(b)
    rows[0].wait()
    rows[1].wait()

    row_pos = lax.broadcasted_iota(jnp.int32, (ROWS // 2, BLK), 0) % BLK
    key_pos = lax.broadcasted_iota(jnp.int32, (ROWS // 2, BLK), 1)
    all_dscores, all_low = [], []
    for half in range(2):
        heads = slice(half * HEADS_HERE // 2, (half + 1) * HEADS_HERE // 2)
        q = q_ref[b, heads].reshape(ROWS // 2, QW)
        g = g_ref[b, heads].reshape(ROWS // 2, LAT)
        scores = jnp.dot(q, k, preferred_element_type=jnp.float32)
        dprobs = jnp.dot(g, k[:LAT], preferred_element_type=jnp.float32)
        parts = []
        for s in range(NSLOT):
            part = scores[:, s * BLK : (s + 1) * BLK] * (SOFTMAX_SCALE * LOG2E)
            if s == 0:
                part = jnp.where(key_pos <= row_pos, part, MASKED)
            else:
                part = jnp.where(info[b, NSLOT + s] > 0, part, MASKED)
            parts.append(part)
        masked = jnp.concatenate(parts, axis=1)
        top = jnp.max(masked, axis=1, keepdims=True)
        expo = jnp.exp2(masked - top)
        probs = expo * (1.0 / jnp.sum(expo, axis=1, keepdims=True))
        delta = jnp.sum(probs * dprobs, axis=1, keepdims=True)
        all_dscores.append((probs * (dprobs - delta) * SOFTMAX_SCALE).astype(jnp.bfloat16))
        all_low.append(probs.astype(jnp.bfloat16))
    dscores = jnp.concatenate(all_dscores, axis=0)
    low = jnp.concatenate(all_low, axis=0)

    rows[2].wait()
    rows[3].wait()
    qt = jnp.concatenate([qt_ref[b, h] for h in range(HEADS_HERE)], axis=1)
    gt = jnp.concatenate([gt_ref[b, h] for h in range(HEADS_HERE)], axis=1)
    key_part = jnp.dot(qt, dscores, preferred_element_type=jnp.float32)
    value_part = jnp.dot(gt, low, preferred_element_type=jnp.float32)
    for s in range(NSLOT):
        cols = slice(s * BLK, (s + 1) * BLK)
        dest = info[b, 2 * NSLOT + s]
        head = dense[dest, :LAT].astype(jnp.float32) + key_part[:LAT, cols] + value_part[:, cols]
        tail = dense[dest, LAT:].astype(jnp.float32) + key_part[LAT:, cols]
        dense[dest, :LAT] = head.astype(jnp.bfloat16)
        dense[dest, LAT:] = tail.astype(jnp.bfloat16)

    def writes():
        each = 4
        return [
            pltpu.make_async_copy(
                dense.at[pl.ds(at, each)], out.at[pl.ds(at % 16, each)], out_sem
            )
            for at, out in ((i, send if i >= 16 else keep) for i in (16, 20, 24, 28, 0, 4, 8, 12))
        ]

    @pl.when(b == 1)
    def _():
        for write in writes():
            write.start()

    dq = lax.dot_general(
        dscores, k, (((1,), (1,)), ((), ())), preferred_element_type=jnp.float32
    ).astype(jnp.bfloat16)
    for h in range(HEADS_HERE):
        dq_ref[:, h] = dq[h * BLK : (h + 1) * BLK].reshape(8, 16, QW)

    @pl.when(b == 1)
    def _():
        for write in writes():
            write.wait()


def local_grads(info, q, qt, g, gt, pieces):
    hbm = pl.BlockSpec(memory_space=pltpu.HBM)
    return pl.pallas_call(
        kernel,
        grid_spec=pltpu.PrefetchScalarGridSpec(
            num_scalar_prefetch=1,
            grid=(2,),
            in_specs=[hbm] * 6,
            out_specs=[pl.BlockSpec((8, HEADS_HERE, 16, QW), lambda b, info: (b, 0, 0, 0))]
            + [hbm] * 2,
            scratch_shapes=[
                pltpu.VMEM((2, HEADS_HERE, BLK, QW), jnp.bfloat16),
                pltpu.VMEM((2, HEADS_HERE, QW, BLK), jnp.bfloat16),
                pltpu.VMEM((2, HEADS_HERE, BLK, LAT), jnp.bfloat16),
                pltpu.VMEM((2, HEADS_HERE, LAT, BLK), jnp.bfloat16),
                pltpu.VMEM((2, NSLOT, QW, BLK), jnp.bfloat16),
                pltpu.VMEM((QW, NSLOT * BLK), jnp.bfloat16),
                pltpu.VMEM((NB, QW, BLK), jnp.bfloat16),
                pltpu.SemaphoreType.DMA((2, 4)),
                pltpu.SemaphoreType.DMA((2, NSLOT)),
                pltpu.SemaphoreType.DMA,
            ],
        ),
        out_shape=[jax.ShapeDtypeStruct((16, HEADS_HERE, 16, QW), jnp.bfloat16)]
        + [jax.ShapeDtypeStruct((NB // 2, QW, BLK), jnp.bfloat16)] * 2,
        compiler_params=pltpu.CompilerParams(
            dimension_semantics=("arbitrary",), vmem_limit_bytes=58 * MIB
        ),
    )(info, q, qt, g, gt, *pieces)


def neighbour(x=0, y=0, z=0, core=0):
    pairs = []
    shape = dict(SPLIT)
    strides = {}
    step = 1
    for name in reversed(AXES):
        strides[name] = step
        step *= shape[name]
    for zl in range(shape["z_lo"]):
        for px in range(shape["x"]):
            for pc in range(shape["core"]):
                for py in range(shape["y"]):
                    for zh in range(shape["z_hi"]):

                        def index(zz, xx, cc, yy):
                            zz %= shape["z_lo"] * shape["z_hi"]
                            high, low = zz // shape["z_lo"], zz % shape["z_lo"]
                            return (
                                low * strides["z_lo"]
                                + (xx % shape["x"]) * strides["x"]
                                + (cc % 2) * strides["core"]
                                + (yy % shape["y"]) * strides["y"]
                                + high * strides["z_hi"]
                            )

                        zz = zh * shape["z_lo"] + zl
                        pairs.append((index(zz, px, pc, py), index(zz + z, px + x, pc + core, py + y)))
    return pairs


def other_z():
    shape = tuple(size for _, size in SPLIT)
    step = math.prod(shape[1:])
    return [(i, (i + step) % (2 * step)) for i in range(2 * step)]


RIGHT, LEFT = neighbour(x=1), neighbour(x=-1)
ALONG_Y = [neighbour(y=d) for d in range(4)]
UP, DOWN = neighbour(z=1), neighbour(z=-1)
SWAP = neighbour(core=1)
OTHER_Z = other_z()


def move(a, pairs):
    return lax.ppermute(a, AXES, pairs)


def pack_kernel(*refs):
    *pieces, out, sem = refs
    copies, at = [], 0
    for piece in pieces:
        n = piece.shape[0]
        copies.append(pltpu.make_async_copy(piece, out.at[pl.ds(at, n)], sem))
        at += n
    for copy in copies:
        copy.start()
    for copy in copies:
        copy.wait()


def pack(pieces):
    n = sum(piece.shape[0] for piece in pieces)
    return pl.pallas_call(
        pack_kernel,
        in_specs=[pl.BlockSpec(memory_space=pl.ANY)] * len(pieces),
        out_specs=pl.BlockSpec(memory_space=pl.ANY),
        out_shape=jax.ShapeDtypeStruct((n, QW, BLK), jnp.bfloat16),
        scratch_shapes=[pltpu.SemaphoreType.DMA],
        compiler_params=pltpu.CompilerParams(vmem_limit_bytes=4 * MIB),
    )(*pieces)


PLACES = (0, 2, 8, 4, 6, 10, 14, 12)
PIECES = (16, 16)


def copies_kernel(*refs):
    left, right, _, *outs, sem = refs
    parts = left, right, left.at[pl.ds(0, 1)], right.at[pl.ds(1, 1)]
    copies = [pltpu.make_async_copy(part, out, sem) for part, out in zip(parts, outs)]
    for copy in copies:
        copy.start()
    for copy in copies:
        copy.wait()


def copies_after(left, right, after):
    anywhere = pl.BlockSpec(memory_space=pl.ANY)
    return pl.pallas_call(
        copies_kernel,
        in_specs=[anywhere] * 3,
        out_specs=[anywhere] * 4,
        out_shape=[jax.ShapeDtypeStruct((n, QW, BLK), jnp.bfloat16) for n in (2, 2, 1, 1)],
        scratch_shapes=[pltpu.SemaphoreType.DMA],
        compiler_params=pltpu.CompilerParams(vmem_limit_bytes=4 * MIB),
    )(left, right, after)


def gather_keys(own, after):
    from_left, from_right, z_own = move(own, RIGHT), move(own, LEFT), move(own, OTHER_Z)
    from_left, from_right, to_right, to_left = copies_after(from_left, from_right, after)
    far = move(to_right, RIGHT), move(to_left, LEFT)
    z_left, z_right = move(from_left, UP), move(from_right, DOWN)
    z_far = move(far[0], UP), move(far[1], DOWN)
    mine = pack([own, from_right, from_left, z_own, *far, z_right, z_left, *z_far])
    return [mine, move(mine, SWAP)]


SUMS = ((8, 2), (10, 2), (6, 2), (12, 2), (4, 2), (14, 2), (0, 4))


def add_cores_kernel(keep, got, *rest):
    n = len(SUMS)
    outs, (ours, theirs, total, in_sems, out_sem) = rest[:n], rest[n:]
    loads, writes = [], []
    for i, (at, count) in enumerate(SUMS):
        part = pl.ds(at, count)
        loads.append(
            [
                pltpu.make_async_copy(keep.at[part], ours.at[part], in_sems.at[i]),
                pltpu.make_async_copy(got.at[part], theirs.at[part], in_sems.at[n + i]),
            ]
        )
        for load in loads[-1]:
            load.start()
    for i, (at, count) in enumerate(SUMS):
        for load in loads[i]:
            load.wait()
        part = slice(at, at + count)
        added = ours[part].astype(jnp.float32) + theirs[part].astype(jnp.float32)
        total[part] = added.astype(jnp.bfloat16)
        writes.append(pltpu.make_async_copy(total.at[pl.ds(at, count)], outs[i], out_sem))
        writes[-1].start()
    for write in writes:
        write.wait()


def add_cores(keep, got):
    hbm = pl.BlockSpec(memory_space=pltpu.HBM)
    return pl.pallas_call(
        add_cores_kernel,
        in_specs=[hbm, hbm],
        out_specs=[hbm] * len(SUMS),
        scratch_shapes=[pltpu.VMEM((16, QW, BLK), jnp.bfloat16)] * 3
        + [pltpu.SemaphoreType.DMA((2 * len(SUMS),)), pltpu.SemaphoreType.DMA],
        out_shape=[jax.ShapeDtypeStruct((count, QW, BLK), jnp.bfloat16) for _, count in SUMS],
        compiler_params=pltpu.CompilerParams(vmem_limit_bytes=24 * MIB),
    )(keep, got)


def total_of(refs, index):
    return sum(ref[index].astype(jnp.float32) for ref in refs)


def pass_on_kernel(right, from_left, left, from_right, right_out, left_out):
    right_out[...] = total_of((right, from_left), ...).astype(jnp.bfloat16)
    left_out[...] = total_of((left, from_right), ...).astype(jnp.bfloat16)


def pass_on(*parts):
    vmem = pl.BlockSpec(memory_space=pltpu.VMEM)
    return pl.pallas_call(
        pass_on_kernel,
        in_specs=[vmem] * 4,
        out_specs=[vmem] * 2,
        out_shape=[jax.ShapeDtypeStruct((2, QW, BLK), jnp.bfloat16)] * 2,
        compiler_params=pltpu.CompilerParams(vmem_limit_bytes=8 * MIB),
    )(*parts)


def add_x_kernel(y_ref, own, *refs):
    parts, outs, turned = (refs[:2], refs[2:4]), refs[4:8], refs[8]
    for z in range(2):
        for block in range(2):
            total = total_of(parts[z], block) + own[2 * z + block].astype(jnp.float32)
            rows = total.T.astype(jnp.bfloat16)
            turned[2 * block, z] = rows[: BLK // 2]
            turned[2 * block + 1, z] = rows[BLK // 2 :]
    for d in range(4):
        outs[d][...] = turned[(y_ref[0] + d) & 3]


def add_x(my_y, parts):
    vmem = pl.BlockSpec(memory_space=pltpu.VMEM)
    shape = (2, BLK // 2, QW)
    return pl.pallas_call(
        add_x_kernel,
        grid_spec=pltpu.PrefetchScalarGridSpec(
            num_scalar_prefetch=1,
            grid=(),
            in_specs=[vmem] * 5,
            out_specs=[vmem] * 4,
            scratch_shapes=[pltpu.VMEM((4, *shape), jnp.bfloat16)],
        ),
        out_shape=[jax.ShapeDtypeStruct(shape, jnp.bfloat16)] * 4,
        compiler_params=pltpu.CompilerParams(vmem_limit_bytes=16 * MIB),
    )(my_y, *parts)


def add_y_kernel(*refs):
    *parts, out = refs
    out[...] = total_of(parts, ...).astype(jnp.bfloat16)


def add_y(parts):
    vmem = pl.BlockSpec(memory_space=pltpu.VMEM)
    return pl.pallas_call(
        add_y_kernel,
        in_specs=[vmem] * 4,
        out_specs=vmem,
        out_shape=jax.ShapeDtypeStruct((2, BLK // 2, QW), jnp.bfloat16),
        compiler_params=pltpu.CompilerParams(vmem_limit_bytes=8 * MIB),
    )(*parts)


def spread(parts, moves):
    return [parts[0]] + [move(parts[d], moves[d]) for d in (1, 2, 3)]


def on_device(queries, latent, grad_out, advantage, ancestors):
    qt = jnp.transpose(queries, (1, 2, 0))
    own_keys = jnp.swapaxes(latent.reshape(2, BLK, QW), 1, 2)
    q, g, gt = prepare(qt, grad_out, advantage)
    pieces = gather_keys(own_keys, gt)

    my_z, my_x, my_core = (lax.axis_index(name) for name in CTX)
    own = lax.axis_index(CTX) * 2 + jnp.arange(2, dtype=jnp.int32)
    slots = jnp.concatenate([own[:, None], ancestors], axis=1)
    present = (slots >= 0).astype(jnp.int32)
    n = jnp.maximum(slots, 0)
    z, x, c, block = n // 16, (n // 4) % 4, (n // 2) % 2, n % 2
    dz, dx, dc = z ^ my_z, (x - my_x) & 3, c ^ my_core
    offset = dz * 4 + dx
    place = dc * 16 + sum(jnp.where(offset == i, at, 0) for i, at in enumerate(PLACES)) + block
    dest = dc * 16 + dx * 4 + z * 2 + block
    info = jnp.concatenate([place, present, dest], axis=1)

    dq, keep, send = local_grads(info, q, qt, g, gt, pieces)

    far_right, far_left, right, left, right_late, left_late, own = add_cores(keep, move(send, SWAP))
    from_left, from_right = move(far_right, RIGHT), move(far_left, LEFT)
    near = move(right, RIGHT), move(left, LEFT)
    on_right, on_left = pass_on(right_late, from_left, left_late, from_right)
    late = move(on_right, RIGHT), move(on_left, LEFT)
    parts = [own, late[0], near[1], near[0], late[1]]
    parts = spread(add_x(lax.axis_index("y")[None], parts), ALONG_Y)
    rows = add_y(parts).reshape(128, QW)
    rows = lax.all_to_all(rows, ("z_lo", "z_hi"), split_axis=0, concat_axis=0, tiled=True)
    latent_grad = jnp.sum(rows.reshape(8, 16, QW).astype(jnp.float32), axis=0)

    dq = lax.all_to_all(dq, HEAD, split_axis=0, concat_axis=0, tiled=True)
    query_grad = jnp.transpose(dq.reshape(64, 16, QW), (1, 0, 2))
    return query_grad, latent_grad


def solution(mesh):
    fine = Mesh(mesh.devices.reshape(SIZES), AXES)
    in_specs = (P(CTX, HEAD, None), P(CTX, None), P(CTX, HEAD, None), P(CTX), P(CTX, None))
    out_specs = (P(CTX + HEAD, None, None), P(CTX + HEAD, None))
    return jax.shard_map(
        on_device, mesh=fine, in_specs=in_specs, out_specs=out_specs, check_vma=False
    )
```

```python
import functools
import math

import jax
import jax.numpy as jnp
from jax import lax
from jax.experimental import pallas as pl
from jax.experimental.pallas import tpu as pltpu
from jax.sharding import Mesh
from jax.sharding import PartitionSpec as P

LAT = 512
QW = 576
BLK = 128
NSLOT = 9
NB = 32
HEADS_HERE = 4
MIB = 1024 * 1024
ROWS = HEADS_HERE * BLK

SOFTMAX_SCALE = 0.07216878364870322
LOG2E = 1.4426950408889634
MASKED = -1e30

SPLIT = (("z_lo", 2), ("x", 4), ("core", 2), ("y", 4), ("z_hi", 4))
AXES = tuple(name for name, _ in SPLIT)
SIZES = tuple(size for _, size in SPLIT)
CTX = AXES[:3]
HEAD = AXES[3:]


def prepare_kernel(advantage_ref, qt_hbm, grad_hbm, q_hbm, g_hbm, gt_hbm, done, *scratch):
    done[...] = jnp.zeros_like(done)
    qt, grad, q, g, gt, in_sems, out_sem = scratch
    heads = range(HEADS_HERE)
    load_grad = pltpu.make_async_copy(grad_hbm, grad, in_sems.at[HEADS_HERE])
    load_grad.start()
    loads = [pltpu.make_async_copy(qt_hbm.at[h], qt.at[h], in_sems.at[h]) for h in heads]
    for load in loads:
        load.start()
    writes = []

    def write(value, hbm, h):
        writes.append(pltpu.make_async_copy(value.at[h], hbm.at[h], out_sem))
        writes[-1].start()

    load_grad.wait()
    for h in heads:
        weighted = grad[:, h, :].T.astype(jnp.float32) * advantage_ref[...]
        gt[h] = weighted.astype(jnp.bfloat16)
        write(gt, gt_hbm, h)
        g[h] = gt[h].T
        write(g, g_hbm, h)
    for h in heads:
        loads[h].wait()
        q[h] = qt[h].T
        write(q, q_hbm, h)
    for copy in writes:
        copy.wait()


def prepare(qt, grad_out, advantage):
    hbm = pl.BlockSpec(memory_space=pltpu.HBM)
    shapes = (HEADS_HERE, 2 * BLK, QW), (HEADS_HERE, 2 * BLK, LAT), (HEADS_HERE, LAT, 2 * BLK)
    scratch = (qt.shape, grad_out.shape, *shapes)
    return pl.pallas_call(
        prepare_kernel,
        in_specs=[pl.BlockSpec(memory_space=pltpu.VMEM), hbm, hbm],
        out_specs=[hbm] * 3 + [pl.BlockSpec(memory_space=pltpu.VMEM)],
        out_shape=[jax.ShapeDtypeStruct(shape, jnp.bfloat16) for shape in (*shapes, (16, 128))],
        scratch_shapes=[pltpu.VMEM(shape, jnp.bfloat16) for shape in scratch]
        + [pltpu.SemaphoreType.DMA((HEADS_HERE + 1,)), pltpu.SemaphoreType.DMA],
        compiler_params=pltpu.CompilerParams(vmem_limit_bytes=58 * MIB),
    )(advantage[None], qt, grad_out)


def kernel(info, q_hbm, qt_hbm, g_hbm, gt_hbm, *rest):
    pieces, rest = rest[:2], rest[2:]
    dq_ref, keep, send = rest[:3]
    q_ref, qt_ref, g_ref, gt_ref, slots, keys, dense, row_sems, slot_sems, out_sem = rest[3:]
    b = pl.program_id(0)

    def loads(block):
        rows = pl.ds(block * BLK, BLK)
        return [
            pltpu.make_async_copy(q_hbm.at[:, rows], q_ref.at[block], row_sems.at[block, 0]),
            pltpu.make_async_copy(g_hbm.at[:, rows], g_ref.at[block], row_sems.at[block, 1]),
            pltpu.make_async_copy(qt_hbm.at[:, :, rows], qt_ref.at[block], row_sems.at[block, 2]),
            pltpu.make_async_copy(gt_hbm.at[:, :, rows], gt_ref.at[block], row_sems.at[block, 3]),
        ]

    def slot_load(block, s, piece, at):
        return pltpu.make_async_copy(
            piece.at[at], slots.at[block, s], slot_sems.at[block, s]
        )

    @pl.when(b == 0)
    def _():
        for block in range(2):
            for s in range(NSLOT):
                place = info[block, s]
                first = 0
                for piece, count in zip(pieces, PIECES):

                    @pl.when((place >= first) & (place < first + count))
                    def _(piece=piece, first=first, s=s, block=block, place=place):
                        slot_load(block, s, piece, place - first).start()

                    first += count

            for load in loads(block):
                load.start()

        def clear(i, carry):
            dense[i] = jnp.zeros((QW, BLK), jnp.bfloat16)
            return carry

        lax.fori_loop(0, NB, clear, 0)

    for s in range(NSLOT):
        slot_load(b, s, pieces[0], 0).wait()
        keys[:, s * BLK : (s + 1) * BLK] = slots[b, s]
    k = keys[...]
    rows = loads(b)
    rows[0].wait()
    rows[1].wait()

    row_pos = lax.broadcasted_iota(jnp.int32, (ROWS // 2, BLK), 0) % BLK
    key_pos = lax.broadcasted_iota(jnp.int32, (ROWS // 2, BLK), 1)
    all_dscores, all_low = [], []
    for half in range(2):
        heads = slice(half * HEADS_HERE // 2, (half + 1) * HEADS_HERE // 2)
        q = q_ref[b, heads].reshape(ROWS // 2, QW)
        g = g_ref[b, heads].reshape(ROWS // 2, LAT)
        scores = jnp.dot(q, k, preferred_element_type=jnp.float32)
        dprobs = jnp.dot(g, k[:LAT], preferred_element_type=jnp.float32)
        parts = []
        for s in range(NSLOT):
            part = scores[:, s * BLK : (s + 1) * BLK] * (SOFTMAX_SCALE * LOG2E)
            if s == 0:
                part = jnp.where(key_pos <= row_pos, part, MASKED)
            else:
                part = jnp.where(info[b, NSLOT + s] > 0, part, MASKED)
            parts.append(part)
        masked = jnp.concatenate(parts, axis=1)
        top = jnp.max(masked, axis=1, keepdims=True)
        expo = jnp.exp2(masked - top)
        probs = expo * (1.0 / jnp.sum(expo, axis=1, keepdims=True))
        delta = jnp.sum(probs * dprobs, axis=1, keepdims=True)
        all_dscores.append((probs * (dprobs - delta) * SOFTMAX_SCALE).astype(jnp.bfloat16))
        all_low.append(probs.astype(jnp.bfloat16))
    dscores = jnp.concatenate(all_dscores, axis=0)
    low = jnp.concatenate(all_low, axis=0)

    rows[2].wait()
    rows[3].wait()
    qt = jnp.concatenate([qt_ref[b, h] for h in range(HEADS_HERE)], axis=1)
    gt = jnp.concatenate([gt_ref[b, h] for h in range(HEADS_HERE)], axis=1)
    key_part = jnp.dot(qt, dscores, preferred_element_type=jnp.float32)
    value_part = jnp.dot(gt, low, preferred_element_type=jnp.float32)
    for s in range(NSLOT):
        cols = slice(s * BLK, (s + 1) * BLK)
        dest = info[b, 2 * NSLOT + s]
        head = dense[dest, :LAT].astype(jnp.float32) + key_part[:LAT, cols] + value_part[:, cols]
        tail = dense[dest, LAT:].astype(jnp.float32) + key_part[LAT:, cols]
        dense[dest, :LAT] = head.astype(jnp.bfloat16)
        dense[dest, LAT:] = tail.astype(jnp.bfloat16)

    def writes():
        each = 4
        return [
            pltpu.make_async_copy(
                dense.at[pl.ds(at, each)], out.at[pl.ds(at % 16, each)], out_sem
            )
            for at, out in ((i, send if i >= 16 else keep) for i in (16, 20, 24, 28, 0, 4, 8, 12))
        ]

    @pl.when(b == 1)
    def _():
        for write in writes():
            write.start()

    dq = lax.dot_general(
        dscores, k, (((1,), (1,)), ((), ())), preferred_element_type=jnp.float32
    ).astype(jnp.bfloat16)
    for h in range(HEADS_HERE):
        dq_ref[:, h] = dq[h * BLK : (h + 1) * BLK].reshape(8, 16, QW)

    @pl.when(b == 1)
    def _():
        for write in writes():
            write.wait()


def local_grads(info, q, qt, g, gt, pieces):
    hbm = pl.BlockSpec(memory_space=pltpu.HBM)
    return pl.pallas_call(
        kernel,
        grid_spec=pltpu.PrefetchScalarGridSpec(
            num_scalar_prefetch=1,
            grid=(2,),
            in_specs=[hbm] * 6,
            out_specs=[pl.BlockSpec((8, HEADS_HERE, 16, QW), lambda b, info: (b, 0, 0, 0))]
            + [hbm] * 2,
            scratch_shapes=[
                pltpu.VMEM((2, HEADS_HERE, BLK, QW), jnp.bfloat16),
                pltpu.VMEM((2, HEADS_HERE, QW, BLK), jnp.bfloat16),
                pltpu.VMEM((2, HEADS_HERE, BLK, LAT), jnp.bfloat16),
                pltpu.VMEM((2, HEADS_HERE, LAT, BLK), jnp.bfloat16),
                pltpu.VMEM((2, NSLOT, QW, BLK), jnp.bfloat16),
                pltpu.VMEM((QW, NSLOT * BLK), jnp.bfloat16),
                pltpu.VMEM((NB, QW, BLK), jnp.bfloat16),
                pltpu.SemaphoreType.DMA((2, 4)),
                pltpu.SemaphoreType.DMA((2, NSLOT)),
                pltpu.SemaphoreType.DMA,
            ],
        ),
        out_shape=[jax.ShapeDtypeStruct((16, HEADS_HERE, 16, QW), jnp.bfloat16)]
        + [jax.ShapeDtypeStruct((NB // 2, QW, BLK), jnp.bfloat16)] * 2,
        compiler_params=pltpu.CompilerParams(
            dimension_semantics=("arbitrary",), vmem_limit_bytes=58 * MIB
        ),
    )(info, q, qt, g, gt, *pieces)


def neighbour(x=0, y=0, z=0, core=0):
    pairs = []
    shape = dict(SPLIT)
    strides = {}
    step = 1
    for name in reversed(AXES):
        strides[name] = step
        step *= shape[name]
    for zl in range(shape["z_lo"]):
        for px in range(shape["x"]):
            for pc in range(shape["core"]):
                for py in range(shape["y"]):
                    for zh in range(shape["z_hi"]):

                        def index(zz, xx, cc, yy):
                            zz %= shape["z_lo"] * shape["z_hi"]
                            high, low = zz // shape["z_lo"], zz % shape["z_lo"]
                            return (
                                low * strides["z_lo"]
                                + (xx % shape["x"]) * strides["x"]
                                + (cc % 2) * strides["core"]
                                + (yy % shape["y"]) * strides["y"]
                                + high * strides["z_hi"]
                            )

                        zz = zh * shape["z_lo"] + zl
                        pairs.append((index(zz, px, pc, py), index(zz + z, px + x, pc + core, py + y)))
    return pairs


def other_z():
    shape = tuple(size for _, size in SPLIT)
    step = math.prod(shape[1:])
    return [(i, (i + step) % (2 * step)) for i in range(2 * step)]


RIGHT, LEFT = neighbour(x=1), neighbour(x=-1)
ALONG_Y = [neighbour(y=d) for d in range(4)]
UP, DOWN = neighbour(z=1), neighbour(z=-1)
RIGHT_UP, LEFT_DOWN = neighbour(x=1, z=1), neighbour(x=-1, z=-1)
SWAP = neighbour(core=1)
OTHER_Z = other_z()


def move(a, pairs):
    return lax.ppermute(a, AXES, pairs)


def key_blocks(piece):
    return [piece.at[:, pl.ds(at, BLK)] for at in range(0, piece.shape[1], BLK)]


def pack_kernel(*refs):
    *pieces, out, sem = refs
    views = [view for piece in pieces for view in key_blocks(piece)]
    copies = [pltpu.make_async_copy(view, out.at[at], sem) for at, view in enumerate(views)]
    for copy in copies:
        copy.start()
    for copy in copies:
        copy.wait()


def pack(pieces):
    n = sum(piece.shape[1] // BLK for piece in pieces)
    return pl.pallas_call(
        pack_kernel,
        in_specs=[pl.BlockSpec(memory_space=pl.ANY)] * len(pieces),
        out_specs=pl.BlockSpec(memory_space=pl.ANY),
        out_shape=jax.ShapeDtypeStruct((n, QW, BLK), jnp.bfloat16),
        scratch_shapes=[pltpu.SemaphoreType.DMA],
        compiler_params=pltpu.CompilerParams(vmem_limit_bytes=4 * MIB),
    )(*pieces)


PLACES = (0, 2, 8, 4, 6, 10, 14, 12)
PIECES = (16, 16)


def copies_kernel(*refs):
    left, right, _, *outs, sem = refs
    parts = left, right, key_blocks(left)[0], key_blocks(right)[1]
    copies = [pltpu.make_async_copy(part, out, sem) for part, out in zip(parts, outs)]
    for copy in copies:
        copy.start()
    for copy in copies:
        copy.wait()


def copies_after(left, right, after):
    anywhere = pl.BlockSpec(memory_space=pl.ANY)
    return pl.pallas_call(
        copies_kernel,
        in_specs=[anywhere] * 3,
        out_specs=[anywhere] * 4,
        out_shape=[jax.ShapeDtypeStruct((QW, n * BLK), jnp.bfloat16) for n in (2, 2, 1, 1)],
        scratch_shapes=[pltpu.SemaphoreType.DMA],
        compiler_params=pltpu.CompilerParams(vmem_limit_bytes=4 * MIB),
    )(left, right, after)


def gather_keys(own, after):
    from_left, from_right, z_own = move(own, RIGHT), move(own, LEFT), move(own, OTHER_Z)
    from_left, from_right, to_right, to_left = copies_after(from_left, from_right, after)
    far = move(to_right, RIGHT), move(to_left, LEFT)
    z_left, z_right = move(from_left, UP), move(from_right, DOWN)
    z_far = move(to_right, RIGHT_UP), move(to_left, LEFT_DOWN)
    mine = pack([own, from_right, from_left, z_own, *far, z_right, z_left, *z_far])
    return [mine, move(mine, SWAP)]


SUMS = ((8, 2), (10, 2), (6, 2), (12, 2), (4, 2), (14, 2), (0, 4))


def add_cores_kernel(keep, got, *rest):
    n = len(SUMS)
    outs, (ours, theirs, total, in_sems, out_sem) = rest[:n], rest[n:]
    loads, writes = [], []
    for i, (at, count) in enumerate(SUMS):
        part = pl.ds(at, count)
        loads.append(
            [
                pltpu.make_async_copy(keep.at[part], ours.at[part], in_sems.at[i]),
                pltpu.make_async_copy(got.at[part], theirs.at[part], in_sems.at[n + i]),
            ]
        )
        for load in loads[-1]:
            load.start()
    for i, (at, count) in enumerate(SUMS):
        for load in loads[i]:
            load.wait()
        part = slice(at, at + count)
        added = ours[part].astype(jnp.float32) + theirs[part].astype(jnp.float32)
        total[part] = added.astype(jnp.bfloat16)
        writes.append(pltpu.make_async_copy(total.at[pl.ds(at, count)], outs[i], out_sem))
        writes[-1].start()
    for write in writes:
        write.wait()


def add_cores(keep, got):
    hbm = pl.BlockSpec(memory_space=pltpu.HBM)
    return pl.pallas_call(
        add_cores_kernel,
        in_specs=[hbm, hbm],
        out_specs=[hbm] * len(SUMS),
        scratch_shapes=[pltpu.VMEM((16, QW, BLK), jnp.bfloat16)] * 3
        + [pltpu.SemaphoreType.DMA((2 * len(SUMS),)), pltpu.SemaphoreType.DMA],
        out_shape=[jax.ShapeDtypeStruct((count, QW, BLK), jnp.bfloat16) for _, count in SUMS],
        compiler_params=pltpu.CompilerParams(vmem_limit_bytes=24 * MIB),
    )(keep, got)


def total_of(refs, index):
    return sum(ref[index].astype(jnp.float32) for ref in refs)


def pass_on_kernel(right, from_left, left, from_right, right_out, left_out):
    right_out[...] = total_of((right, from_left), ...).astype(jnp.bfloat16)
    left_out[...] = total_of((left, from_right), ...).astype(jnp.bfloat16)


def pass_on(*parts):
    vmem = pl.BlockSpec(memory_space=pltpu.VMEM)
    return pl.pallas_call(
        pass_on_kernel,
        in_specs=[vmem] * 4,
        out_specs=[vmem] * 2,
        out_shape=[jax.ShapeDtypeStruct((2, QW, BLK), jnp.bfloat16)] * 2,
        compiler_params=pltpu.CompilerParams(vmem_limit_bytes=8 * MIB),
    )(*parts)


def add_x_kernel(y_ref, own, *refs):
    parts, outs, turned = (refs[:2], refs[2:4]), refs[4:8], refs[8]
    for z in range(2):
        for block in range(2):
            total = total_of(parts[z], block) + own[2 * z + block].astype(jnp.float32)
            rows = total.T.astype(jnp.bfloat16)
            cols = slice(z * QW, (z + 1) * QW)
            turned[2 * block, :, cols] = rows[: BLK // 2]
            turned[2 * block + 1, :, cols] = rows[BLK // 2 :]
    for d in range(4):
        outs[d][...] = turned[(y_ref[0] + d) & 3]


def add_x(my_y, parts):
    vmem = pl.BlockSpec(memory_space=pltpu.VMEM)
    shape = (BLK // 2, 2 * QW)
    return pl.pallas_call(
        add_x_kernel,
        grid_spec=pltpu.PrefetchScalarGridSpec(
            num_scalar_prefetch=1,
            grid=(),
            in_specs=[vmem] * 5,
            out_specs=[vmem] * 4,
            scratch_shapes=[pltpu.VMEM((4, *shape), jnp.bfloat16)],
        ),
        out_shape=[jax.ShapeDtypeStruct(shape, jnp.bfloat16)] * 4,
        compiler_params=pltpu.CompilerParams(vmem_limit_bytes=16 * MIB),
    )(my_y, *parts)


def add_y_kernel(*refs):
    *parts, out = refs
    total = total_of(parts, ...).astype(jnp.bfloat16)
    out[0] = total[:, :QW]
    out[1] = total[:, QW:]


def add_y(parts):
    vmem = pl.BlockSpec(memory_space=pltpu.VMEM)
    return pl.pallas_call(
        add_y_kernel,
        in_specs=[vmem] * 4,
        out_specs=vmem,
        out_shape=jax.ShapeDtypeStruct((2, BLK // 2, QW), jnp.bfloat16),
        compiler_params=pltpu.CompilerParams(vmem_limit_bytes=8 * MIB),
    )(*parts)


def spread(parts, moves):
    return [parts[0]] + [move(parts[d], moves[d]) for d in (1, 2, 3)]


def on_device(queries, latent, grad_out, advantage, ancestors):
    qt = jnp.transpose(queries, (1, 2, 0))
    q, g, gt, done = prepare(qt, grad_out, advantage)
    pieces = gather_keys(latent.T, done)

    my_z, my_x, my_core = (lax.axis_index(name) for name in CTX)
    own = lax.axis_index(CTX) * 2 + jnp.arange(2, dtype=jnp.int32)
    slots = jnp.concatenate([own[:, None], ancestors], axis=1)
    present = (slots >= 0).astype(jnp.int32)
    n = jnp.maximum(slots, 0)
    z, x, c, block = n // 16, (n // 4) % 4, (n // 2) % 2, n % 2
    dz, dx, dc = z ^ my_z, (x - my_x) & 3, c ^ my_core
    offset = dz * 4 + dx
    place = dc * 16 + sum(jnp.where(offset == i, at, 0) for i, at in enumerate(PLACES)) + block
    dest = dc * 16 + dx * 4 + z * 2 + block
    info = jnp.concatenate([place, present, dest], axis=1)

    dq, keep, send = local_grads(info, q, qt, g, gt, pieces)

    far_right, far_left, right, left, right_late, left_late, own = add_cores(keep, move(send, SWAP))
    from_left, from_right = move(far_right, RIGHT), move(far_left, LEFT)
    near = move(right, RIGHT), move(left, LEFT)
    on_right, on_left = pass_on(right_late, from_left, left_late, from_right)
    late = move(on_right, RIGHT), move(on_left, LEFT)
    parts = [own, late[0], near[1], near[0], late[1]]
    parts = spread(add_x(lax.axis_index("y")[None], parts), ALONG_Y)
    rows = add_y(parts).reshape(128, QW)
    rows = lax.all_to_all(rows, ("z_lo", "z_hi"), split_axis=0, concat_axis=0, tiled=True)
    latent_grad = jnp.sum(rows.reshape(8, 16, QW).astype(jnp.float32), axis=0)

    dq = lax.all_to_all(dq, HEAD, split_axis=0, concat_axis=0, tiled=True)
    query_grad = jnp.transpose(dq.reshape(64, 16, QW), (1, 0, 2))
    return query_grad, latent_grad


def solution(mesh):
    fine = Mesh(mesh.devices.reshape(SIZES), AXES)
    in_specs = (P(CTX, HEAD, None), P(CTX, None), P(CTX, HEAD, None), P(CTX), P(CTX, None))
    out_specs = (P(CTX + HEAD, None, None), P(CTX + HEAD, None))
    return jax.shard_map(
        on_device, mesh=fine, in_specs=in_specs, out_specs=out_specs, check_vma=False
    )
```

```python
import functools
import math

import jax
import jax.numpy as jnp
from jax import lax
from jax.experimental import pallas as pl
from jax.experimental.pallas import tpu as pltpu
from jax.sharding import Mesh
from jax.sharding import PartitionSpec as P

LAT = 512
QW = 576
BLK = 128
NSLOT = 9
NB = 32
HEADS_HERE = 4
MIB = 1024 * 1024
ROWS = HEADS_HERE * BLK

SOFTMAX_SCALE = 0.07216878364870322
LOG2E = 1.4426950408889634
MASKED = -1e30

SPLIT = (("z_lo", 2), ("x", 4), ("core", 2), ("y", 4), ("z_hi", 4))
AXES = tuple(name for name, _ in SPLIT)
SIZES = tuple(size for _, size in SPLIT)
CTX = AXES[:3]
HEAD = AXES[3:]


def prepare_kernel(advantage_ref, qt_hbm, grad_hbm, q_hbm, g_hbm, gt_hbm, done, *scratch):
    done[...] = jnp.zeros_like(done)
    qt, grad, q, g, gt, in_sems, out_sem = scratch
    heads = range(HEADS_HERE)
    load_grad = pltpu.make_async_copy(grad_hbm, grad, in_sems.at[HEADS_HERE])
    load_grad.start()
    loads = [pltpu.make_async_copy(qt_hbm.at[h], qt.at[h], in_sems.at[h]) for h in heads]
    for load in loads:
        load.start()
    writes = []

    def write(value, hbm, h):
        writes.append(pltpu.make_async_copy(value.at[h], hbm.at[h], out_sem))
        writes[-1].start()

    load_grad.wait()
    for h in heads:
        weighted = grad[:, h, :].T.astype(jnp.float32) * advantage_ref[...]
        gt[h] = weighted.astype(jnp.bfloat16)
        write(gt, gt_hbm, h)
        g[h] = gt[h].T
        write(g, g_hbm, h)
    for h in heads:
        loads[h].wait()
        q[h] = qt[h].T
        write(q, q_hbm, h)
    for copy in writes:
        copy.wait()


def prepare(qt, grad_out, advantage):
    hbm = pl.BlockSpec(memory_space=pltpu.HBM)
    shapes = (HEADS_HERE, 2 * BLK, QW), (HEADS_HERE, 2 * BLK, LAT), (HEADS_HERE, LAT, 2 * BLK)
    scratch = (qt.shape, grad_out.shape, *shapes)
    return pl.pallas_call(
        prepare_kernel,
        in_specs=[pl.BlockSpec(memory_space=pltpu.VMEM), hbm, hbm],
        out_specs=[hbm] * 3 + [pl.BlockSpec(memory_space=pltpu.VMEM)],
        out_shape=[jax.ShapeDtypeStruct(shape, jnp.bfloat16) for shape in (*shapes, (16, 128))],
        scratch_shapes=[pltpu.VMEM(shape, jnp.bfloat16) for shape in scratch]
        + [pltpu.SemaphoreType.DMA((HEADS_HERE + 1,)), pltpu.SemaphoreType.DMA],
        compiler_params=pltpu.CompilerParams(vmem_limit_bytes=58 * MIB),
    )(advantage[None], qt, grad_out)


def kernel(info, q_hbm, qt_hbm, g_hbm, gt_hbm, *rest):
    pieces, rest = rest[:2], rest[2:]
    dq_ref, keep, send = rest[:3]
    q_ref, qt_ref, g_ref, gt_ref, slots, keys, dense, row_sems, slot_sems, out_sem = rest[3:]
    b = pl.program_id(0)

    def loads(block):
        rows = pl.ds(block * BLK, BLK)
        return [
            pltpu.make_async_copy(q_hbm.at[:, rows], q_ref.at[block], row_sems.at[block, 0]),
            pltpu.make_async_copy(g_hbm.at[:, rows], g_ref.at[block], row_sems.at[block, 1]),
            pltpu.make_async_copy(qt_hbm.at[:, :, rows], qt_ref.at[block], row_sems.at[block, 2]),
            pltpu.make_async_copy(gt_hbm.at[:, :, rows], gt_ref.at[block], row_sems.at[block, 3]),
        ]

    def slot_load(block, s, piece, at):
        return pltpu.make_async_copy(
            piece.at[at], slots.at[block, s], slot_sems.at[block, s]
        )

    @pl.when(b == 0)
    def _():
        for block in range(2):
            for s in range(NSLOT):
                place = info[block, s]
                first = 0
                for piece, count in zip(pieces, PIECES):

                    @pl.when((place >= first) & (place < first + count))
                    def _(piece=piece, first=first, s=s, block=block, place=place):
                        slot_load(block, s, piece, place - first).start()

                    first += count

            for load in loads(block):
                load.start()

        def clear(i, carry):
            dense[i] = jnp.zeros((QW, BLK), jnp.bfloat16)
            return carry

        lax.fori_loop(0, NB, clear, 0)

    for s in range(NSLOT):
        slot_load(b, s, pieces[0], 0).wait()
        keys[:, s * BLK : (s + 1) * BLK] = slots[b, s]
    k = keys[...]
    rows = loads(b)
    rows[0].wait()
    rows[1].wait()

    key_pos = lax.broadcasted_iota(jnp.int32, (32, BLK), 1)
    row_pos = lax.broadcasted_iota(jnp.int32, (32, BLK), 0)
    shown = [info[b, NSLOT + s] > 0 for s in range(NSLOT)]
    all_dscores, all_low = [], []
    for half in range(2):
        heads = slice(half * HEADS_HERE // 2, (half + 1) * HEADS_HERE // 2)
        q = q_ref[b, heads].reshape(ROWS // 2, QW)
        g = g_ref[b, heads].reshape(ROWS // 2, LAT)
        scores = jnp.dot(q, k, preferred_element_type=jnp.float32)
        dprobs = jnp.dot(g, k[:LAT], preferred_element_type=jnp.float32)
        for at in range(0, ROWS // 2, 32):
            parts = []
            for s in range(NSLOT):
                part = scores[at : at + 32, s * BLK : (s + 1) * BLK] * (SOFTMAX_SCALE * LOG2E)
                if s == 0:
                    part = jnp.where(key_pos <= row_pos + at % BLK, part, MASKED)
                else:
                    part = jnp.where(shown[s], part, MASKED)
                parts.append(part)
            top = jnp.max(functools.reduce(jnp.maximum, parts), axis=1, keepdims=True)
            expo = [jnp.exp2(part - top) for part in parts]
            inverse = 1.0 / jnp.sum(sum(expo), axis=1, keepdims=True)
            grads = [dprobs[at : at + 32, s * BLK : (s + 1) * BLK] for s in range(NSLOT)]
            delta = jnp.sum(sum(e * d for e, d in zip(expo, grads)), axis=1, keepdims=True)
            delta = delta * inverse
            probs = [e * inverse for e in expo]
            low = [p.astype(jnp.bfloat16) for p in probs]
            ds = [(p * (d - delta) * SOFTMAX_SCALE).astype(jnp.bfloat16) for p, d in zip(probs, grads)]
            all_low.append(jnp.concatenate(low, axis=1))
            all_dscores.append(jnp.concatenate(ds, axis=1))
    dscores = jnp.concatenate(all_dscores, axis=0)
    low = jnp.concatenate(all_low, axis=0)

    rows[2].wait()
    rows[3].wait()
    qt = jnp.concatenate([qt_ref[b, h] for h in range(HEADS_HERE)], axis=1)
    gt = jnp.concatenate([gt_ref[b, h] for h in range(HEADS_HERE)], axis=1)
    key_part = jnp.dot(qt, dscores, preferred_element_type=jnp.float32)
    value_part = jnp.dot(gt, low, preferred_element_type=jnp.float32)
    for s in range(NSLOT):
        cols = slice(s * BLK, (s + 1) * BLK)
        dest = info[b, 2 * NSLOT + s]
        head = dense[dest, :LAT].astype(jnp.float32) + key_part[:LAT, cols] + value_part[:, cols]
        tail = dense[dest, LAT:].astype(jnp.float32) + key_part[LAT:, cols]
        dense[dest, :LAT] = head.astype(jnp.bfloat16)
        dense[dest, LAT:] = tail.astype(jnp.bfloat16)

    def writes():
        each = 4
        return [
            pltpu.make_async_copy(
                dense.at[pl.ds(at, each)], out.at[pl.ds(at % 16, each)], out_sem
            )
            for at, out in ((i, send if i >= 16 else keep) for i in (16, 20, 24, 28, 0, 4, 8, 12))
        ]

    @pl.when(b == 1)
    def _():
        for write in writes():
            write.start()

    dq = lax.dot_general(
        dscores, k, (((1,), (1,)), ((), ())), preferred_element_type=jnp.float32
    ).astype(jnp.bfloat16)
    for h in range(HEADS_HERE):
        dq_ref[:, h] = dq[h * BLK : (h + 1) * BLK].reshape(8, 16, QW)

    @pl.when(b == 1)
    def _():
        for write in writes():
            write.wait()


def local_grads(info, q, qt, g, gt, pieces):
    hbm = pl.BlockSpec(memory_space=pltpu.HBM)
    return pl.pallas_call(
        kernel,
        grid_spec=pltpu.PrefetchScalarGridSpec(
            num_scalar_prefetch=1,
            grid=(2,),
            in_specs=[hbm] * 6,
            out_specs=[pl.BlockSpec((8, HEADS_HERE, 16, QW), lambda b, info: (b, 0, 0, 0))]
            + [hbm] * 2,
            scratch_shapes=[
                pltpu.VMEM((2, HEADS_HERE, BLK, QW), jnp.bfloat16),
                pltpu.VMEM((2, HEADS_HERE, QW, BLK), jnp.bfloat16),
                pltpu.VMEM((2, HEADS_HERE, BLK, LAT), jnp.bfloat16),
                pltpu.VMEM((2, HEADS_HERE, LAT, BLK), jnp.bfloat16),
                pltpu.VMEM((2, NSLOT, QW, BLK), jnp.bfloat16),
                pltpu.VMEM((QW, NSLOT * BLK), jnp.bfloat16),
                pltpu.VMEM((NB, QW, BLK), jnp.bfloat16),
                pltpu.SemaphoreType.DMA((2, 4)),
                pltpu.SemaphoreType.DMA((2, NSLOT)),
                pltpu.SemaphoreType.DMA,
            ],
        ),
        out_shape=[jax.ShapeDtypeStruct((16, HEADS_HERE, 16, QW), jnp.bfloat16)]
        + [jax.ShapeDtypeStruct((NB // 2, QW, BLK), jnp.bfloat16)] * 2,
        compiler_params=pltpu.CompilerParams(
            dimension_semantics=("arbitrary",), vmem_limit_bytes=58 * MIB
        ),
    )(info, q, qt, g, gt, *pieces)


def neighbour(x=0, y=0, z=0, core=0):
    pairs = []
    shape = dict(SPLIT)
    strides = {}
    step = 1
    for name in reversed(AXES):
        strides[name] = step
        step *= shape[name]
    for zl in range(shape["z_lo"]):
        for px in range(shape["x"]):
            for pc in range(shape["core"]):
                for py in range(shape["y"]):
                    for zh in range(shape["z_hi"]):

                        def index(zz, xx, cc, yy):
                            zz %= shape["z_lo"] * shape["z_hi"]
                            high, low = zz // shape["z_lo"], zz % shape["z_lo"]
                            return (
                                low * strides["z_lo"]
                                + (xx % shape["x"]) * strides["x"]
                                + (cc % 2) * strides["core"]
                                + (yy % shape["y"]) * strides["y"]
                                + high * strides["z_hi"]
                            )

                        zz = zh * shape["z_lo"] + zl
                        pairs.append((index(zz, px, pc, py), index(zz + z, px + x, pc + core, py + y)))
    return pairs


def other_z():
    shape = tuple(size for _, size in SPLIT)
    step = math.prod(shape[1:])
    return [(i, (i + step) % (2 * step)) for i in range(2 * step)]


RIGHT, LEFT = neighbour(x=1), neighbour(x=-1)
ALONG_Y = [neighbour(y=d) for d in range(4)]
UP, DOWN = neighbour(z=1), neighbour(z=-1)
RIGHT_UP, LEFT_DOWN = neighbour(x=1, z=1), neighbour(x=-1, z=-1)
SWAP = neighbour(core=1)
OTHER_Z = other_z()


def move(a, pairs):
    return lax.ppermute(a, AXES, pairs)


def key_blocks(piece):
    return [piece.at[:, pl.ds(at, BLK)] for at in range(0, piece.shape[1], BLK)]


def pack_kernel(*refs):
    *pieces, out, sem = refs
    views = [view for piece in pieces for view in key_blocks(piece)]
    copies = [pltpu.make_async_copy(view, out.at[at], sem) for at, view in enumerate(views)]
    for copy in copies:
        copy.start()
    for copy in copies:
        copy.wait()


def pack(pieces):
    n = sum(piece.shape[1] // BLK for piece in pieces)
    return pl.pallas_call(
        pack_kernel,
        in_specs=[pl.BlockSpec(memory_space=pl.ANY)] * len(pieces),
        out_specs=pl.BlockSpec(memory_space=pl.ANY),
        out_shape=jax.ShapeDtypeStruct((n, QW, BLK), jnp.bfloat16),
        scratch_shapes=[pltpu.SemaphoreType.DMA],
        compiler_params=pltpu.CompilerParams(vmem_limit_bytes=4 * MIB),
    )(*pieces)


PLACES = (0, 2, 8, 4, 6, 10, 14, 12)
PIECES = (16, 16)


def copies_kernel(*refs):
    left, right, _, *outs, sem = refs
    parts = left, right, key_blocks(left)[0], key_blocks(right)[1]
    copies = [pltpu.make_async_copy(part, out, sem) for part, out in zip(parts, outs)]
    for copy in copies:
        copy.start()
    for copy in copies:
        copy.wait()


def copies_after(left, right, after):
    anywhere = pl.BlockSpec(memory_space=pl.ANY)
    return pl.pallas_call(
        copies_kernel,
        in_specs=[anywhere] * 3,
        out_specs=[anywhere] * 4,
        out_shape=[jax.ShapeDtypeStruct((QW, n * BLK), jnp.bfloat16) for n in (2, 2, 1, 1)],
        scratch_shapes=[pltpu.SemaphoreType.DMA],
        compiler_params=pltpu.CompilerParams(vmem_limit_bytes=4 * MIB),
    )(left, right, after)


def gather_keys(own, after):
    from_left, from_right, z_own = move(own, RIGHT), move(own, LEFT), move(own, OTHER_Z)
    from_left, from_right, to_right, to_left = copies_after(from_left, from_right, after)
    far = move(to_right, RIGHT), move(to_left, LEFT)
    z_left, z_right = move(from_left, UP), move(from_right, DOWN)
    z_far = move(to_right, RIGHT_UP), move(to_left, LEFT_DOWN)
    mine = pack([own, from_right, from_left, z_own, *far, z_right, z_left, *z_far])
    return [mine, move(mine, SWAP)]


SUMS = ((8, 2), (10, 2), (6, 2), (12, 2), (4, 2), (14, 2), (0, 4))


def add_cores_kernel(keep, got, *rest):
    n = len(SUMS)
    outs, (ours, theirs, total, in_sems, out_sem) = rest[:n], rest[n:]
    loads, writes = [], []
    for i, (at, count) in enumerate(SUMS):
        part = pl.ds(at, count)
        loads.append(
            [
                pltpu.make_async_copy(keep.at[part], ours.at[part], in_sems.at[i]),
                pltpu.make_async_copy(got.at[part], theirs.at[part], in_sems.at[n + i]),
            ]
        )
        for load in loads[-1]:
            load.start()
    for i, (at, count) in enumerate(SUMS):
        for load in loads[i]:
            load.wait()
        part = slice(at, at + count)
        added = ours[part].astype(jnp.float32) + theirs[part].astype(jnp.float32)
        total[part] = added.astype(jnp.bfloat16)
        writes.append(pltpu.make_async_copy(total.at[pl.ds(at, count)], outs[i], out_sem))
        writes[-1].start()
    for write in writes:
        write.wait()


def add_cores(keep, got):
    hbm = pl.BlockSpec(memory_space=pltpu.HBM)
    return pl.pallas_call(
        add_cores_kernel,
        in_specs=[hbm, hbm],
        out_specs=[hbm] * len(SUMS),
        scratch_shapes=[pltpu.VMEM((16, QW, BLK), jnp.bfloat16)] * 3
        + [pltpu.SemaphoreType.DMA((2 * len(SUMS),)), pltpu.SemaphoreType.DMA],
        out_shape=[jax.ShapeDtypeStruct((count, QW, BLK), jnp.bfloat16) for _, count in SUMS],
        compiler_params=pltpu.CompilerParams(vmem_limit_bytes=24 * MIB),
    )(keep, got)


def total_of(refs, index):
    return sum(ref[index].astype(jnp.float32) for ref in refs)


def pass_on_kernel(right, from_left, left, from_right, right_out, left_out):
    right_out[...] = total_of((right, from_left), ...).astype(jnp.bfloat16)
    left_out[...] = total_of((left, from_right), ...).astype(jnp.bfloat16)


def pass_on(*parts):
    vmem = pl.BlockSpec(memory_space=pltpu.VMEM)
    return pl.pallas_call(
        pass_on_kernel,
        in_specs=[vmem] * 4,
        out_specs=[vmem] * 2,
        out_shape=[jax.ShapeDtypeStruct((2, QW, BLK), jnp.bfloat16)] * 2,
        compiler_params=pltpu.CompilerParams(vmem_limit_bytes=8 * MIB),
    )(*parts)


def add_x_kernel(y_ref, own, *refs):
    parts, outs, turned = (refs[:2], refs[2:4]), refs[4:8], refs[8]
    for z in range(2):
        for block in range(2):
            total = total_of(parts[z], block) + own[2 * z + block].astype(jnp.float32)
            rows = total.T.astype(jnp.bfloat16)
            cols = slice(z * QW, (z + 1) * QW)
            turned[2 * block, :, cols] = rows[: BLK // 2]
            turned[2 * block + 1, :, cols] = rows[BLK // 2 :]
    for d in range(4):
        outs[d][...] = turned[(y_ref[0] + d) & 3]


def add_x(my_y, parts):
    vmem = pl.BlockSpec(memory_space=pltpu.VMEM)
    shape = (BLK // 2, 2 * QW)
    return pl.pallas_call(
        add_x_kernel,
        grid_spec=pltpu.PrefetchScalarGridSpec(
            num_scalar_prefetch=1,
            grid=(),
            in_specs=[vmem] * 5,
            out_specs=[vmem] * 4,
            scratch_shapes=[pltpu.VMEM((4, *shape), jnp.bfloat16)],
        ),
        out_shape=[jax.ShapeDtypeStruct(shape, jnp.bfloat16)] * 4,
        compiler_params=pltpu.CompilerParams(vmem_limit_bytes=16 * MIB),
    )(my_y, *parts)


def add_y_kernel(*refs):
    *parts, out = refs
    total = total_of(parts, ...).astype(jnp.bfloat16)
    out[0] = total[:, :QW]
    out[1] = total[:, QW:]


def add_y(parts):
    vmem = pl.BlockSpec(memory_space=pltpu.VMEM)
    return pl.pallas_call(
        add_y_kernel,
        in_specs=[vmem] * 4,
        out_specs=vmem,
        out_shape=jax.ShapeDtypeStruct((2, BLK // 2, QW), jnp.bfloat16),
        compiler_params=pltpu.CompilerParams(vmem_limit_bytes=8 * MIB),
    )(*parts)


def spread(parts, moves):
    far = move(parts[2], moves[2])
    return [parts[0], move(parts[1], moves[1]), far, move(parts[3], moves[3])]


def on_device(queries, latent, grad_out, advantage, ancestors):
    qt = jnp.transpose(queries, (1, 2, 0))
    q, g, gt, done = prepare(qt, grad_out, advantage)
    pieces = gather_keys(latent.T, done)

    my_z, my_x, my_core = (lax.axis_index(name) for name in CTX)
    own = lax.axis_index(CTX) * 2 + jnp.arange(2, dtype=jnp.int32)
    slots = jnp.concatenate([own[:, None], ancestors], axis=1)
    present = (slots >= 0).astype(jnp.int32)
    n = jnp.maximum(slots, 0)
    z, x, c, block = n // 16, (n // 4) % 4, (n // 2) % 2, n % 2
    dz, dx, dc = z ^ my_z, (x - my_x) & 3, c ^ my_core
    offset = dz * 4 + dx
    place = dc * 16 + sum(jnp.where(offset == i, at, 0) for i, at in enumerate(PLACES)) + block
    dest = dc * 16 + dx * 4 + z * 2 + block
    info = jnp.concatenate([place, present, dest], axis=1)

    dq, keep, send = local_grads(info, q, qt, g, gt, pieces)

    far_right, far_left, right, left, right_late, left_late, own = add_cores(keep, move(send, SWAP))
    from_left, from_right = move(far_right, RIGHT), move(far_left, LEFT)
    near = move(right, RIGHT), move(left, LEFT)
    on_right, on_left = pass_on(right_late, from_left, left_late, from_right)
    late = move(on_right, RIGHT), move(on_left, LEFT)
    parts = [own, late[0], near[1], near[0], late[1]]
    parts = spread(add_x(lax.axis_index("y")[None], parts), ALONG_Y)
    rows = add_y(parts).reshape(128, QW)
    rows = lax.all_to_all(rows, ("z_lo", "z_hi"), split_axis=0, concat_axis=0, tiled=True)
    latent_grad = jnp.sum(rows.reshape(8, 16, QW).astype(jnp.float32), axis=0)

    dq = lax.all_to_all(dq, HEAD, split_axis=0, concat_axis=0, tiled=True)
    query_grad = jnp.transpose(dq.reshape(64, 16, QW), (1, 0, 2))
    return query_grad, latent_grad


def solution(mesh):
    fine = Mesh(mesh.devices.reshape(SIZES), AXES)
    in_specs = (P(CTX, HEAD, None), P(CTX, None), P(CTX, HEAD, None), P(CTX), P(CTX, None))
    out_specs = (P(CTX + HEAD, None, None), P(CTX + HEAD, None))
    return jax.shard_map(
        on_device, mesh=fine, in_specs=in_specs, out_specs=out_specs, check_vma=False
    )
```
